512 devices in a mesh: tower: 2 (over core), tp: 16 (over z), grp: 16 (over y, x).
Axes of the slice: x: 4, y: 4, z: 16, core: 2. Of those that a mesh axis runs over, the one named last changes fastest.
Arguments:
- tokens: bfloat16 [12288, 8192], P('grp', 'tp'), may hold values from -700 to 700
- modality: int32 [12288], P('grp'), may hold values from 0 to 1, as said below
- doc_ids: int32 [12288], P('grp'), may hold values from 0 to 255, as said below
- owner_ids: int32 [12288], P('grp'), may hold values from 0 to 15, as said below
- norm_gain: float32 [2, 8192], P('tower'), may hold values from 0.5 to 1.5
- query_weight: bfloat16 [2, 8192, 4096], P('tower', 'grp', 'tp'), may hold values from -0.125 to 0.125
- pair_weight: bfloat16 [2, 8192, 1024], P('tower', 'grp'), may hold values from -0.125 to 0.125
Outputs:
- attended: bfloat16 [2, 12288, 4096], P('tower', 'grp', 'tp')
The draws below stay inside these ranges and needn't reach their ends.
Inputs may be any that keep to these rules, and one draw needn't show every extreme that they name: Every group of 768 tokens holds exactly 384 tokens of each modality. `owner_ids`: within every group each owner is named by exactly 48 tokens, and by at most 48 tokens of one modality. `doc_ids`: all tokens of one document have the same owner.
All inputs are finite; a program needn't handle non-finite values.
Results may differ from the reference program's by a relative error of at most 0.0084.
Values may be sent and summed in bfloat16 or wider, within the bound.
No kernel may reach another device: no remote copies, remote signals or barrier semaphores. Data moves between devices by JAX's collectives and lax.ppermute only.
A program may use at most 64 MiB of HBM per device.

```python
import math
import jax
import jax.numpy as jnp
from jax import lax

D = 8192
HD = 128
HEADS = 32
KV_HEADS = 4
TOK = 768
GROUPS = 16
SLOT = 48
TOKENS = 12288


WEIGHT_EDGE = 0.125


def layout(key):
    base_key = jax.random.fold_in(key, 1234)
    perm_key, run_key, star_key, cut_key = jax.random.split(base_key, 4)
    permuted = jax.vmap(lambda subkey: jax.random.permutation(subkey, TOK))(jax.random.split(perm_key, GROUPS)).astype(jnp.int32)
    owner_table = permuted // SLOT
    position = jnp.arange(TOK, dtype=jnp.int32)
    sorted_order = jnp.argsort(owner_table * TOK + position[None, :], axis=1).astype(jnp.int32)
    placed = jnp.argsort(sorted_order, axis=1).astype(jnp.int32)
    within = placed % SLOT
    first_half = jax.random.randint(run_key, (GROUPS, GROUPS // 2), 0, SLOT + 1)
    star_owner = jax.random.randint(star_key, (), 0, GROUPS)
    forced = jnp.where(star_owner % 2 == 0, SLOT, 0)
    first_half = jnp.where(jnp.arange(GROUPS // 2)[None, :] == star_owner // 2, forced, first_half)
    image_run = jnp.stack([first_half, SLOT - first_half], axis=2).reshape(GROUPS, GROUPS)
    run_here = jnp.take_along_axis(image_run, owner_table, axis=1)
    modality_table = (within < run_here).astype(jnp.int32)
    cut_flags = (jax.random.randint(cut_key, (GROUPS, GROUPS), 0, 4) == 0).astype(jnp.int32)
    cut_flags = cut_flags.at[GROUPS - 1, :].set(1)
    cut_flags = cut_flags.at[:, 0].set(0)
    segment = jnp.cumsum(cut_flags, axis=1)
    doc_table = owner_table * GROUPS + jnp.take_along_axis(segment.T, owner_table, axis=1)
    return (modality_table.reshape(-1), doc_table.reshape(-1).astype(jnp.int32), owner_table.reshape(-1))


def column_scale(key):
    return jnp.exp(jax.random.uniform(jax.random.fold_in(key, 77), (D,), jnp.float32, 0.0, math.log(10.0)))


def draw_modality(key, part):
    return layout(key)[0]


def draw_doc_ids(key, part):
    return layout(key)[1]


def draw_owner_ids(key, part):
    return layout(key)[2]


def draw_tokens(key, part):
    row_key, noise_key = jax.random.split(jax.random.fold_in(key, 11), 2)
    columns = column_scale(key)
    row_scales = jnp.exp(jax.random.uniform(row_key, (TOKENS, 1), jnp.float32, 0.0, math.log(10.0)))
    base_draw = jax.random.normal(noise_key, (TOKENS, D), jnp.float32)
    drawn = base_draw * row_scales * columns[None, :]
    return jnp.clip(drawn, -700.0, 700.0).astype(jnp.bfloat16)


def draw_query_weight(key, part):
    drawn = jax.random.normal(jax.random.fold_in(key, 21), (2, D, HEADS * HD), jnp.float32) / math.sqrt(D)
    return jnp.clip(drawn, -WEIGHT_EDGE, WEIGHT_EDGE).astype(jnp.bfloat16)


def draw_pair_weight(key, part):
    drawn = jax.random.normal(jax.random.fold_in(key, 31), (2, D, KV_HEADS, 2, HD), jnp.float32) / math.sqrt(D)
    return jnp.clip(drawn, -WEIGHT_EDGE, WEIGHT_EDGE).reshape(2, D, KV_HEADS * 2 * HD).astype(jnp.bfloat16)


def setup_inputs(seed: int = 0) -> dict:
    seeds = jax.random.split(jax.random.key(seed), 8)
    return {
        "tokens": draw_tokens(jax.random.fold_in(seeds[7], 71), 0),
        "modality": draw_modality(jax.random.fold_in(seeds[7], 71), 0),
        "doc_ids": draw_doc_ids(jax.random.fold_in(seeds[7], 71), 0),
        "owner_ids": draw_owner_ids(jax.random.fold_in(seeds[7], 71), 0),
        "norm_gain": jnp.clip(1.0 + 0.1 * jax.random.normal(seeds[4], (2, D), jnp.float32), 0.5, 1.5),
        "query_weight": draw_query_weight(jax.random.fold_in(seeds[7], 71), 0),
        "pair_weight": draw_pair_weight(jax.random.fold_in(seeds[7], 71), 0),
    }


EPS = 1e-05
MASKED = -1e+30

def normalize(rows, gain_row):
    values = rows.astype(jnp.float32)
    inverse_rms = lax.rsqrt(lax.optimization_barrier(jnp.mean(values * values, axis=1, keepdims=True)) + EPS)
    return (values * inverse_rms * gain_row[None, :]).astype(jnp.bfloat16)

def reference(tokens, modality, doc_ids, owner_ids, norm_gain, query_weight, pair_weight):
    query_all = jnp.zeros((TOKENS, HEADS * HD), jnp.bfloat16)
    pair_all = jnp.zeros((TOKENS, KV_HEADS * 2 * HD), jnp.bfloat16)
    for tower_index in range(2):
        picked = jnp.nonzero(modality == tower_index, size=TOKENS // 2)[0].astype(jnp.int32)
        normed = normalize(tokens[picked], norm_gain[tower_index])
        query_rows = jnp.dot(normed, query_weight[tower_index], preferred_element_type=jnp.float32).astype(jnp.bfloat16)
        pair_rows = jnp.dot(normed, pair_weight[tower_index], preferred_element_type=jnp.float32).astype(jnp.bfloat16)
        query_all = query_all.at[picked].set(query_rows)
        pair_all = pair_all.at[picked].set(pair_rows)
    sharing = HEADS // KV_HEADS
    scale_factor = 1.0 / math.sqrt(HD)

    def attend(owner_index):
        members = jnp.nonzero(owner_ids == owner_index, size=TOK)[0].astype(jnp.int32)
        queries = query_all[members].astype(jnp.float32).reshape(TOK, KV_HEADS, sharing, HD)
        pair_data = pair_all[members].astype(jnp.float32).reshape(TOK, KV_HEADS, 2, HD)
        doc_rows = doc_ids[members]
        images = modality[members] == 1
        allowed = (doc_rows[:, None] == doc_rows[None, :]) & ((members[None, :] <= members[:, None]) | images[:, None] & images[None, :])
        scores = jnp.einsum('qjgd,kjd->jgqk', queries, pair_data[:, :, 0]) * scale_factor
        scores = jnp.where(allowed[None, None], scores, MASKED)
        row_max = lax.optimization_barrier(jnp.max(scores, axis=3, keepdims=True))
        powered = jnp.exp(scores - row_max)
        weights = (powered / lax.optimization_barrier(jnp.sum(powered, axis=3, keepdims=True))).astype(jnp.bfloat16)
        mixed_rows = jnp.einsum('jgqk,kjd->qjgd', weights.astype(jnp.float32), pair_data[:, :, 1])
        return (mixed_rows.astype(jnp.bfloat16).reshape(TOK, HEADS * HD), members)
    outputs, member_lists = lax.map(attend, jnp.arange(GROUPS, dtype=jnp.int32))
    attention = jnp.zeros((TOKENS, HEADS * HD), jnp.bfloat16).at[member_lists.reshape(-1)].set(outputs.reshape(TOKENS, HEADS * HD))
    towers = jnp.arange(2, dtype=jnp.int32)
    return jnp.where(modality[None, :, None] == towers[:, None, None], attention[None], jnp.zeros((), jnp.bfloat16))
```

```python
import functools
import math

import jax
import jax.numpy as jnp
from jax import lax
from jax.experimental import pallas as pl
from jax.experimental.pallas import tpu as pltpu
from jax.sharding import PartitionSpec as P

HD = 128
EPS = 1e-05
MASKED = -1e30
LIFT = 64.0
MIB = 2**20
BF16, F32, I32 = jnp.bfloat16, jnp.float32, jnp.int32
VMEM = pl.BlockSpec(memory_space=pltpu.VMEM)
ANY = pl.BlockSpec(memory_space=pl.ANY)


def iota(shape, dim):
    return lax.broadcasted_iota(I32, shape, dim)


def ones_where(mask):
    return jnp.where(mask, 1.0, 0.0).astype(BF16)


def dot(a, b):
    return jnp.dot(a, b, preferred_element_type=F32)


def dot_nt(a, b):
    return lax.dot_general(a, b, (((1,), (1,)), ((), ())), preferred_element_type=F32)


def fold(parts):
    return functools.reduce(lambda a, b: a + b, parts)


def split_number(value):
    high = lax.shift_right_logical(value, 5)
    return high.astype(F32), (value - 32 * high).astype(F32)


def stack_rows(rows):
    shape = (8, rows[0].shape[1])
    at = iota(shape, 0)
    return fold(jnp.where(at == k, row, 0.0) for k, row in enumerate(rows)).astype(BF16)


def prepare_kernel(
    groups, pair_heads, modality_ref, owner_ref, doc_ref, token_ref, query_ref, pair_ref,
    chosen_ref, info_ref, packed_ref, spread_ref, block, sems,
):
    tok = token_ref.shape[0]
    half = chosen_ref.shape[0]
    slots = tok // groups
    rows, head_cols = query_ref.shape[1:]
    cols = head_cols + HD
    tower = lax.axis_index("tower")
    rank = lax.axis_index("tp")
    per_head = lax.axis_size("tp") // pair_heads
    column = (rank // per_head) * 2 * HD + (rank % 2) * HD
    loads = (
        pltpu.make_async_copy(
            query_ref.at[0], block.at[pl.ds(0, rows), pl.ds(0, head_cols)], sems.at[2 * groups]
        ),
        pltpu.make_async_copy(
            pair_ref.at[0, :, pl.ds(pl.multiple_of(column, HD), HD)],
            block.at[pl.ds(0, rows), pl.ds(head_cols, HD)],
            sems.at[2 * groups + 1],
        ),
    )
    for copy in loads:
        copy.start()
    for copy in loads:
        copy.wait()
    weights = [
        pltpu.make_async_copy(
            block.at[pl.ds(0, rows)], spread_ref.at[g, pl.ds(0, rows)], sems.at[g]
        )
        for g in range(groups)
    ]
    for copy in weights:
        copy.start()

    modality, owner = modality_ref[...], owner_ref[...]
    match = iota((groups, tok), 0) == owner
    text = jnp.where(match & (modality == 0), 1.0, 0.0)
    image = jnp.where(match & (modality == 1), 1.0, 0.0)
    both = jnp.concatenate([text, image], axis=0)
    before = ones_where(iota((tok, tok), 0) < iota((tok, tok), 1))
    counts = dot(both.astype(BF16), before)
    in_owner = counts * both
    text_slot = jnp.sum(in_owner[:groups], axis=0, keepdims=True)
    image_slot = (slots - 1.0) - jnp.sum(in_owner[groups:], axis=0, keepdims=True)
    slot = jnp.where(modality == 1, image_slot, text_slot).astype(I32)
    dest = owner * slots + slot
    text_rank = jnp.sum(counts[:groups], axis=0, keepdims=True)
    image_rank = jnp.sum(counts[groups:], axis=0, keepdims=True)
    in_tower = modality == tower
    own_rank = jnp.where(modality == 1, image_rank, text_rank).astype(I32)
    own_rank = jnp.where(in_tower, own_rank, half)
    select = ones_where(iota((half, tok), 0) == own_rank)
    chosen_ref[...] = dot(select, token_ref[...]).astype(BF16)

    at = iota((8, tok), 0)
    info_ref[...] = jnp.where(at == 0, dest, jnp.where(at == 1, in_tower.astype(I32), 0))
    high, low = split_number(dest)
    packed = dot_nt(stack_rows([high, low]), select)
    packed_ref[...] = (32.0 * packed[0:1] + packed[1:2]).astype(I32) + iota((8, half), 0) * 0

    high, low = split_number(iota((1, tok), 1))
    facts = stack_rows([doc_ref[...].astype(F32), high, low, modality.astype(F32)])
    table = dot_nt(facts, ones_where(iota((tok, tok), 0) == dest))
    if tok < cols:
        table = jnp.concatenate([table, jnp.zeros((8, 2 * cols - tok), F32)], axis=1)
    block[rows : rows + 16, :] = jnp.concatenate(
        [table[:, :cols], table[:, cols:]], axis=0
    ).astype(BF16)
    notes = [
        pltpu.make_async_copy(
            block.at[pl.ds(rows, 16)], spread_ref.at[g, pl.ds(rows, 16)], sems.at[groups + g]
        )
        for g in range(groups)
    ]
    for copy in notes:
        copy.start()
    for copy in weights + notes:
        copy.wait()


def prepare(modality, owner_ids, doc_ids, tokens, query_weight, pair_weight, groups):
    tok, slab = tokens.shape
    rows, head_cols = query_weight.shape[1:]
    half, cols = tok // 2, head_cols + HD
    kernel = functools.partial(prepare_kernel, groups, pair_weight.shape[2] // (2 * HD))
    return pl.pallas_call(
        kernel,
        out_shape=(
            jax.ShapeDtypeStruct((half, slab), BF16),
            jax.ShapeDtypeStruct((8, tok), I32),
            jax.ShapeDtypeStruct((8, half), I32),
            jax.ShapeDtypeStruct((groups, rows + 16, cols), BF16),
        ),
        in_specs=[VMEM, VMEM, VMEM, VMEM, ANY, ANY],
        out_specs=(VMEM, VMEM, VMEM, ANY),
        scratch_shapes=[
            pltpu.VMEM((rows + 16, cols), BF16),
            pltpu.SemaphoreType.DMA((2 * groups + 2,)),
        ],
        compiler_params=pltpu.CompilerParams(vmem_limit_bytes=32 * MIB),
        name="prepare",
    )(modality[None], owner_ids[None], doc_ids[None], tokens, query_weight, pair_weight)


def project_kernel(width, feature_ref, weight_ref, gain_ref, query_ref, pair_ref, total, squares):
    step = pl.program_id(0)

    @pl.when(step == 0)
    def _():
        total[...] = jnp.zeros_like(total)
        squares[...] = jnp.zeros_like(squares)

    values = feature_ref[0].astype(F32)
    squared = values * values
    slab = values.shape[1]
    squares[...] += fold(squared[:, c : c + HD] for c in range(0, slab, HD))
    scaled = (values * gain_ref[...]).astype(BF16)
    total[...] += dot(scaled, weight_ref[0])

    @pl.when(step == pl.num_programs(0) - 1)
    def _():
        mean = jnp.sum(squares[...], axis=1, keepdims=True) * (1.0 / width)
        rows = total[...] * lax.rsqrt(mean + EPS)
        head_cols = query_ref.shape[1]
        query_ref[...] = rows[:, :head_cols].astype(BF16)
        pair_ref[...] = rows[:, head_cols:].astype(BF16)


def project(features, weights, gain):
    count, half, slab = features.shape
    groups, _, cols = weights.shape
    rows = weights.shape[1] - 16
    head_cols = cols - HD
    assert groups * rows == count * slab and rows == slab
    return pl.pallas_call(
        functools.partial(project_kernel, count * slab),
        grid=(count,),
        out_shape=(
            jax.ShapeDtypeStruct((half, head_cols), BF16),
            jax.ShapeDtypeStruct((half, HD), BF16),
        ),
        in_specs=[
            pl.BlockSpec((1, half, slab), lambda k: (k, 0, 0)),
            pl.BlockSpec((1, rows, cols), lambda k: (k, 0, 0)),
            pl.BlockSpec((1, slab), lambda k: (0, k)),
        ],
        out_specs=(
            pl.BlockSpec((half, head_cols), lambda k: (0, 0)),
            pl.BlockSpec((half, HD), lambda k: (0, 0)),
        ),
        scratch_shapes=[pltpu.VMEM((half, cols), F32), pltpu.VMEM((half, HD), F32)],
        compiler_params=pltpu.CompilerParams(vmem_limit_bytes=24 * MIB),
        name="project",
    )(features, weights, gain)


def place_kernel(packed_ref, query_ref, mine_ref, other_ref, out_ref):
    tok, half = out_ref.shape[1], query_ref.shape[0]
    place = ones_where(iota((tok, half), 0) == packed_ref[0:1, :])
    queries = dot(place, query_ref[...]).astype(BF16)
    mine = dot(place, mine_ref[...]).astype(BF16)
    other = dot(place, other_ref[...]).astype(BF16)
    for core in range(2):
        out_ref[core, :, :HD] = queries[:, core * HD : (core + 1) * HD]

    def pair(keys, values):
        for core in range(2):
            out_ref[core, :, HD : 2 * HD] = keys
            out_ref[core, :, 2 * HD :] = values

    even = lax.axis_index("tp") % 2 == 0

    @pl.when(even)
    def _():
        pair(mine, other)

    @pl.when(jnp.logical_not(even))
    def _():
        pair(other, mine)


def place(packed, query_rows, mine, other, tok):
    return pl.pallas_call(
        place_kernel,
        out_shape=jax.ShapeDtypeStruct((2, tok, 3 * HD), BF16),
        in_specs=[VMEM] * 4,
        out_specs=VMEM,
        compiler_params=pltpu.CompilerParams(vmem_limit_bytes=24 * MIB),
        name="place",
    )(packed, query_rows, mine, other)


def mask_kernel(tok, note_ref, info_ref, bias_ref, back_ref):
    groups, _, cols = note_ref.shape
    slots = tok // groups
    group = lax.axis_index("grp")
    notes = note_ref[...].astype(F32)
    facts = jnp.concatenate([notes[:, :8], notes[:, 8:]], axis=2)[:, :, :tok]
    facts = facts.reshape(groups * 8, tok).astype(BF16)

    def part(index):
        return jnp.floor((index.astype(F32) + 0.5) * (1.0 / slots))

    column = iota((1, tok), 1)
    from_group = part(column)
    slot = column - slots * from_group.astype(I32)
    take = ones_where(iota((tok, tok), 0) == group * slots + slot)
    seen = dot(facts, take).reshape(groups, 8, tok)
    at = iota((groups, 8, tok), 0)
    rows = jnp.sum(jnp.where(at == from_group.astype(I32)[None], seen, 0.0), axis=0)
    same = ones_where(iota((tok, tok), 0) == iota((tok, tok), 1))
    turned = dot_nt(same, rows.astype(BF16))
    row_place = tok * from_group + 32.0 * rows[1:2] + rows[2:3]
    turned_place = tok * part(iota((tok, 1), 0)) + 32.0 * turned[:, 1:2] + turned[:, 2:3]
    after = (row_place <= turned_place) | (rows[3:4] * turned[:, 3:4] > 0.5)
    allowed = (rows[0:1] == turned[:, 0:1]) & after
    bias_ref[...] = jnp.where(allowed, 0.0, MASKED).astype(BF16)

    high, low = split_number(info_ref[0:1, :])
    back = dot_nt(same, stack_rows([high, low, info_ref[1:2, :].astype(F32)]))
    dest = (32.0 * back[:, 0:1] + back[:, 1:2]).astype(I32)
    dest = jnp.where(back[:, 2:3] > 0.5, dest, -1)
    back_ref[...] = ones_where(iota((tok, tok), 1) == dest)


def masks(weights, info):
    tok = info.shape[1]
    groups, rows, cols = weights.shape
    at = rows // 16 - 1
    return pl.pallas_call(
        functools.partial(mask_kernel, tok),
        grid=(1,),
        out_shape=(
            jax.ShapeDtypeStruct((tok, tok), BF16),
            jax.ShapeDtypeStruct((tok, tok), BF16),
        ),
        in_specs=[
            pl.BlockSpec((groups, 16, cols), lambda k: (0, at, 0)),
            pl.BlockSpec((8, tok), lambda k: (0, 0)),
        ],
        out_specs=(
            pl.BlockSpec((tok, tok), lambda k: (0, 0)),
            pl.BlockSpec((tok, tok), lambda k: (0, 0)),
        ),
        compiler_params=pltpu.CompilerParams(vmem_limit_bytes=40 * MIB),
        name="masks",
    )(weights, info)


def attend_kernel(given_ref, bias_ref, out_ref):
    tok = given_ref.shape[1]
    merged = given_ref[0] + given_ref[1]
    keys, values = merged[:, HD : 2 * HD], merged[:, 2 * HD :]
    tile = min(256, tok)
    for at in range(0, tok, tile):
        scores = dot_nt(merged[at : at + tile, :HD], keys) * (1.0 / math.sqrt(HD))
        scores = scores + bias_ref[at : at + tile, :].astype(F32)
        powered = jnp.exp(scores - jnp.max(scores, axis=1, keepdims=True))
        inverse = 1.0 / jnp.sum(powered, axis=1, keepdims=True)
        mixed = dot((powered * inverse).astype(BF16), values).astype(BF16)
        out_ref[0, at : at + tile, :] = mixed
        out_ref[1, at : at + tile, :] = mixed


def attend(given, bias):
    tok = bias.shape[0]
    return pl.pallas_call(
        attend_kernel,
        out_shape=jax.ShapeDtypeStruct((2, tok, HD), BF16),
        in_specs=[VMEM, VMEM],
        out_specs=VMEM,
        compiler_params=pltpu.CompilerParams(vmem_limit_bytes=32 * MIB),
        name="attend",
    )(given, bias)


def restore_kernel(back_ref, given_ref, out_ref):
    for core in range(2):
        out_ref[0, :, core * HD : (core + 1) * HD] = dot(back_ref[...], given_ref[core]).astype(BF16)


def restore(back, given):
    tok = back.shape[0]
    return pl.pallas_call(
        restore_kernel,
        out_shape=jax.ShapeDtypeStruct((1, tok, 2 * HD), BF16),
        in_specs=[VMEM, VMEM],
        out_specs=VMEM,
        compiler_params=pltpu.CompilerParams(vmem_limit_bytes=24 * MIB),
        name="restore",
    )(back, given)


def swap_all(value, axes):
    return lax.all_to_all(value, axes, split_axis=0, concat_axis=0, tiled=True)


def local(tokens, modality, doc_ids, owner_ids, norm_gain, query_weight, pair_weight):
    groups = lax.axis_size("grp")
    tok = tokens.shape[0]
    slots = tok // groups
    chosen, info, packed, spread = prepare(
        modality, owner_ids, doc_ids, tokens, query_weight, pair_weight, groups
    )
    weights = swap_all(spread, "grp")
    lifted = (chosen.astype(F32) * LIFT).astype(jnp.float16)
    gathered = lax.all_gather(lifted, "tp", axis=0)
    features = (gathered.astype(F32) * (1.0 / LIFT)).astype(BF16)
    query_rows, mine = project(features, weights, norm_gain)
    pairs = [(t, t ^ 1) for t in range(lax.axis_size("tp"))]
    other = lax.ppermute(mine, "tp", pairs)
    sent = place(packed, query_rows, mine, other, tok)
    weights, info, sent = lax.optimization_barrier((weights, info, sent))
    given = swap_all(sent.reshape(2 * groups, slots, 3 * HD), ("tower", "grp"))
    bias, back = masks(weights, info)
    mixed = attend(given.reshape(2, tok, 3 * HD), bias)
    returned = swap_all(mixed.reshape(2 * groups, slots, HD), ("tower", "grp"))
    return restore(back, returned.reshape(2, tok, HD))


def solution(mesh):
    in_specs = (
        P("grp", "tp"),
        P("grp"),
        P("grp"),
        P("grp"),
        P("tower", None),
        P("tower", "grp", "tp"),
        P("tower", "grp", None),
    )
    out_specs = P("tower", "grp", "tp")
    return jax.shard_map(local, mesh=mesh, in_specs=in_specs, out_specs=out_specs, check_vma=False)
```

```python
import functools
import math

import jax
import jax.numpy as jnp
from jax import lax
from jax.experimental import pallas as pl
from jax.experimental.pallas import tpu as pltpu
from jax.sharding import PartitionSpec as P

HD = 128
EPS = 1e-05
MASKED = -1e30
LIFT = 64.0
MIB = 2**20
BF16, F32, I32 = jnp.bfloat16, jnp.float32, jnp.int32
VMEM = pl.BlockSpec(memory_space=pltpu.VMEM)
HBM = pl.BlockSpec(memory_space=pltpu.HBM)


def iota(shape, dim):
    return lax.broadcasted_iota(I32, shape, dim)


def ones_where(mask):
    return jnp.where(mask, 1.0, 0.0).astype(BF16)


def dot(a, b):
    return jnp.dot(a, b, preferred_element_type=F32)


def dot_nt(a, b):
    return lax.dot_general(a, b, (((1,), (1,)), ((), ())), preferred_element_type=F32)


def fold(parts):
    return functools.reduce(lambda a, b: a + b, parts)


def split_number(value):
    high = lax.shift_right_logical(value, 5)
    return high.astype(F32), (value - 32 * high).astype(F32)


def stack_rows(rows):
    shape = (8, rows[0].shape[1])
    at = iota(shape, 0)
    return fold(jnp.where(at == k, row, 0.0) for k, row in enumerate(rows)).astype(BF16)


def slots_of(modality, owner, groups):
    tok = owner.shape[1]
    slots = tok // groups
    match = iota((groups, tok), 0) == owner
    text = jnp.where(match & (modality == 0), 1.0, 0.0)
    image = jnp.where(match & (modality == 1), 1.0, 0.0)
    both = jnp.concatenate([text, image], axis=0)
    before = ones_where(iota((tok, tok), 0) < iota((tok, tok), 1))
    counts = dot(both.astype(BF16), before)
    in_owner = counts * both
    text_slot = jnp.sum(in_owner[:groups], axis=0, keepdims=True)
    image_slot = (slots - 1.0) - jnp.sum(in_owner[groups:], axis=0, keepdims=True)
    slot = jnp.where(modality == 1, image_slot, text_slot).astype(I32)
    text_rank = jnp.sum(counts[:groups], axis=0, keepdims=True)
    image_rank = jnp.sum(counts[groups:], axis=0, keepdims=True)
    rank = jnp.where(modality == 1, image_rank, text_rank).astype(I32)
    return owner * slots + slot, rank


def row_of(ref):
    return ref[...].reshape(1, ref.shape[0])


def in_hbm(*arrays):
    return tuple(pltpu.with_memory_space_constraint(a, pltpu.HBM) for a in arrays)


def pack_kernel(
    groups, pair_heads, modality_ref, owner_ref, doc_ref, query_ref, pair_ref,
    spread_ref, block, modality_own, owner_own, doc_own, sems,
):
    tok = modality_ref.shape[0]
    rows, head_cols = query_ref.shape[1:]
    cols = head_cols + HD
    rank = lax.axis_index("tp")
    per_head = lax.axis_size("tp") // pair_heads
    column = (rank // per_head) * 2 * HD + (rank % 2) * HD
    sources = (
        (query_ref.at[0], block.at[pl.ds(0, rows), pl.ds(0, head_cols)]),
        (
            pair_ref.at[0, :, pl.ds(pl.multiple_of(column, HD), HD)],
            block.at[pl.ds(0, rows), pl.ds(head_cols, HD)],
        ),
        (modality_ref, modality_own),
        (owner_ref, owner_own),
        (doc_ref, doc_own),
    )
    loads = [
        pltpu.make_async_copy(source, target, sems.at[2 * groups + k])
        for k, (source, target) in enumerate(sources)
    ]
    for copy in loads:
        copy.start()
    for copy in loads[:2]:
        copy.wait()
    weights = [
        pltpu.make_async_copy(
            block.at[pl.ds(0, rows)], spread_ref.at[g, pl.ds(0, rows)], sems.at[g]
        )
        for g in range(groups)
    ]
    for copy in weights:
        copy.start()
    for copy in loads[2:]:
        copy.wait()
    modality = row_of(modality_own)
    dest, _ = slots_of(modality, row_of(owner_own), groups)
    high, low = split_number(iota((1, tok), 1))
    facts = stack_rows([row_of(doc_own).astype(F32), high, low, modality.astype(F32)])
    table = dot_nt(facts, ones_where(iota((tok, tok), 0) == dest))
    if tok < 2 * cols:
        table = jnp.concatenate([table, jnp.zeros((8, 2 * cols - tok), F32)], axis=1)
    block[rows : rows + 16, :] = jnp.concatenate(
        [table[:, :cols], table[:, cols:]], axis=0
    ).astype(BF16)
    notes = [
        pltpu.make_async_copy(
            block.at[pl.ds(rows, 16)], spread_ref.at[g, pl.ds(rows, 16)], sems.at[groups + g]
        )
        for g in range(groups)
    ]
    for copy in notes:
        copy.start()
    for copy in weights + notes:
        copy.wait()


def pack(modality, owner_ids, doc_ids, query_weight, pair_weight, groups):
    tok = modality.shape[0]
    rows, head_cols = query_weight.shape[1:]
    cols = head_cols + HD
    kernel = functools.partial(pack_kernel, groups, pair_weight.shape[2] // (2 * HD))
    return pl.pallas_call(
        kernel,
        out_shape=pltpu.HBM((groups, rows + 16, cols), BF16),
        in_specs=[HBM] * 5,
        out_specs=HBM,
        scratch_shapes=[
            pltpu.VMEM((rows + 16, cols), BF16),
            pltpu.VMEM((tok,), I32),
            pltpu.VMEM((tok,), I32),
            pltpu.VMEM((tok,), I32),
            pltpu.SemaphoreType.DMA((2 * groups + 5,)),
        ],
        compiler_params=pltpu.CompilerParams(vmem_limit_bytes=16 * MIB),
        name="pack",
    )(*in_hbm(modality, owner_ids, doc_ids, query_weight, pair_weight))


def choose_kernel(modality_ref, token_ref, chosen_ref, modality_own, token_own, sems):
    tok, half = token_ref.shape[0], chosen_ref.shape[0]
    loads = (
        pltpu.make_async_copy(modality_ref, modality_own, sems.at[0]),
        pltpu.make_async_copy(token_ref, token_own, sems.at[1]),
    )
    for copy in loads:
        copy.start()
    loads[0].wait()
    mine = row_of(modality_own) == lax.axis_index("tower")
    before = ones_where(iota((tok, tok), 0) < iota((tok, tok), 1))
    flags = jnp.broadcast_to(jnp.where(mine, 1.0, 0.0), (8, tok)).astype(BF16)
    rank = jnp.where(mine, dot(flags, before)[0:1].astype(I32), half)
    select = ones_where(iota((half, tok), 0) == rank)
    loads[1].wait()
    chosen_ref[...] = dot(select, token_own[...]).astype(BF16)


def choose(modality, tokens):
    tok, slab = tokens.shape
    return pl.pallas_call(
        choose_kernel,
        out_shape=jax.ShapeDtypeStruct((tok // 2, slab), BF16),
        in_specs=[HBM, HBM],
        out_specs=VMEM,
        scratch_shapes=[
            pltpu.VMEM((tok,), I32),
            pltpu.VMEM((tok, slab), BF16),
            pltpu.SemaphoreType.DMA((2,)),
        ],
        compiler_params=pltpu.CompilerParams(vmem_limit_bytes=16 * MIB),
        name="choose",
    )(*in_hbm(modality, tokens))


def normalize_kernel(feature_ref, gain_ref, out_ref):
    count, half, slab = feature_ref.shape
    tile = 48 if half % 48 == 0 else 16

    @pl.loop(0, half // tile)
    def _(step):
        at = pl.ds(pl.multiple_of(step * tile, 16), tile)
        squares = jnp.zeros((tile, HD), F32)
        for k in range(count):
            values = feature_ref[k, at, :].astype(F32)
            squared = values * values
            squares += fold([squared[:, c : c + HD] for c in range(0, slab, HD)])
        mean = jnp.sum(squares, axis=1, keepdims=True) * (1.0 / (count * slab))
        inverse = lax.rsqrt(mean + EPS)
        for k in range(count):
            values = feature_ref[k, at, :].astype(F32) * inverse
            gain = gain_ref[:, k * slab : (k + 1) * slab]
            out_ref[k, at, :] = (values * gain).astype(BF16)


def normalize(features, gain):
    return pl.pallas_call(
        normalize_kernel,
        out_shape=jax.ShapeDtypeStruct(features.shape, BF16),
        in_specs=[VMEM, VMEM],
        out_specs=VMEM,
        compiler_params=pltpu.CompilerParams(vmem_limit_bytes=20 * MIB),
        name="normalize",
    )(features, gain)


def project_kernel(normed_ref, weight_ref, keep_ref, mine_ref, give_ref, rows, block, sems):
    count, _, slab = normed_ref.shape
    loads = []
    for k in range(count):
        loads.append(
            (
                pltpu.make_async_copy(normed_ref.at[k], rows.at[k], sems.at[2 * k]),
                pltpu.make_async_copy(
                    weight_ref.at[k, pl.ds(0, slab)], block.at[k], sems.at[2 * k + 1]
                ),
            )
        )
    for pair in loads:
        for copy in pair:
            copy.start()
    total = None
    together = 2
    for at in range(0, count, together):
        for pair in loads[at : at + together]:
            for copy in pair:
                copy.wait()
        term = fold([dot(rows[k], block[k]) for k in range(at, at + together)])
        total = term if total is None else total + term
    total = total.astype(BF16)
    mine = total[:, 2 * HD :]
    mine_ref[...] = mine
    give_ref[:, HD:] = mine
    text = lax.axis_index("tower") == 0

    @pl.when(text)
    def _():
        keep_ref[...] = total[:, :HD]
        give_ref[:, :HD] = total[:, HD : 2 * HD]

    @pl.when(jnp.logical_not(text))
    def _():
        keep_ref[...] = total[:, HD : 2 * HD]
        give_ref[:, :HD] = total[:, :HD]


def project(normed, weights):
    count, half, slab = normed.shape
    groups, rows, cols = weights.shape
    assert groups == count and rows == slab + 16 and cols == 3 * HD
    return pl.pallas_call(
        project_kernel,
        out_shape=(
            jax.ShapeDtypeStruct((half, HD), BF16),
            jax.ShapeDtypeStruct((half, HD), BF16),
            jax.ShapeDtypeStruct((half, 2 * HD), BF16),
        ),
        in_specs=[HBM, HBM],
        out_specs=(VMEM,) * 3,
        scratch_shapes=[
            pltpu.VMEM((count, half, slab), BF16),
            pltpu.VMEM((count, slab, cols), BF16),
            pltpu.SemaphoreType.DMA((2 * count,)),
        ],
        compiler_params=pltpu.CompilerParams(vmem_limit_bytes=32 * MIB),
        name="project",
    )(*in_hbm(normed, weights))


def plan_kernel(groups, modality_ref, owner_ref, place_ref):
    tok = place_ref.shape[0]
    half = tok // 2
    modality = row_of(modality_ref)
    dest, rank = slots_of(modality, row_of(owner_ref), groups)
    rank = jnp.where(modality == lax.axis_index("tower"), rank, half + rank)
    select = ones_where(iota((tok, tok), 0) == rank)
    high, low = split_number(dest)
    packed = dot_nt(stack_rows([high, low]), select)
    packed = (32.0 * packed[0:1] + packed[1:2]).astype(I32)
    place_ref[...] = ones_where(iota((tok, tok), 0) == packed)


def plan(modality, owner_ids, groups):
    tok = modality.shape[0]
    return pl.pallas_call(
        functools.partial(plan_kernel, groups),
        out_shape=jax.ShapeDtypeStruct((tok, tok), BF16),
        in_specs=[VMEM, VMEM],
        out_specs=VMEM,
        compiler_params=pltpu.CompilerParams(vmem_limit_bytes=24 * MIB),
        name="plan",
    )(modality, owner_ids)


def place_kernel(place_ref, keep_ref, got_ref, mine_ref, out_ref):
    half = keep_ref.shape[0]
    own, other = place_ref[:, :half], place_ref[:, half:]
    out_ref[:, :HD] = (dot(own, keep_ref[...]) + dot(other, got_ref[:, :HD])).astype(BF16)
    out_ref[:, HD:] = (dot(own, mine_ref[...]) + dot(other, got_ref[:, HD:])).astype(BF16)


def place(where, keep, got, mine):
    tok = where.shape[0]
    return pl.pallas_call(
        place_kernel,
        out_shape=jax.ShapeDtypeStruct((tok, 2 * HD), BF16),
        in_specs=[VMEM] * 4,
        out_specs=VMEM,
        compiler_params=pltpu.CompilerParams(vmem_limit_bytes=16 * MIB),
        name="place",
    )(where, keep, got, mine)


def mask_kernel(note_ref, modality_ref, owner_ref, bias_ref, back_ref, notes, sem):
    groups, rows, cols = note_ref.shape
    tok = bias_ref.shape[0]
    slots = tok // groups
    copy = pltpu.make_async_copy(note_ref.at[:, pl.ds(rows - 16, 16)], notes, sem)
    copy.start()
    modality = row_of(modality_ref)
    dest, _ = slots_of(modality, row_of(owner_ref), groups)
    same = ones_where(iota((tok, tok), 0) == iota((tok, tok), 1))
    high, low = split_number(dest)
    mine = jnp.where(modality == lax.axis_index("tower"), 1.0, 0.0)
    back = dot_nt(same, stack_rows([high, low, mine]))
    dest = (32.0 * back[:, 0:1] + back[:, 1:2]).astype(I32)
    dest = jnp.where(back[:, 2:3] > 0.5, dest, -1)
    back_ref[...] = ones_where(iota((tok, tok), 1) == dest)

    copy.wait()
    group = lax.axis_index("grp")
    seen = notes[...].astype(F32)
    facts = jnp.concatenate([seen[:, :8], seen[:, 8:]], axis=2)[:, :, :tok]
    facts = facts.reshape(groups * 8, tok).astype(BF16)

    def part(index):
        return jnp.floor((index.astype(F32) + 0.5) * (1.0 / slots))

    column = iota((1, tok), 1)
    from_group = part(column)
    slot = column - slots * from_group.astype(I32)
    take = ones_where(iota((tok, tok), 0) == group * slots + slot)
    seen = dot(facts, take).reshape(groups, 8, tok)
    at = iota((groups, 8, tok), 0)
    row = jnp.sum(jnp.where(at == from_group.astype(I32)[None], seen, 0.0), axis=0)
    turned = dot_nt(same, row.astype(BF16))
    row_place = tok * from_group + 32.0 * row[1:2] + row[2:3]
    turned_place = tok * part(iota((tok, 1), 0)) + 32.0 * turned[:, 1:2] + turned[:, 2:3]
    after = (row_place <= turned_place) | (row[3:4] * turned[:, 3:4] > 0.5)
    allowed = (row[0:1] == turned[:, 0:1]) & after
    bias_ref[...] = jnp.where(allowed, 0.0, MASKED).astype(BF16)


def masks(weights, modality, owner_ids):
    tok = modality.shape[0]
    groups, _, cols = weights.shape
    return pl.pallas_call(
        mask_kernel,
        out_shape=(
            jax.ShapeDtypeStruct((tok, tok), BF16),
            jax.ShapeDtypeStruct((tok, tok), BF16),
        ),
        in_specs=[HBM, VMEM, VMEM],
        out_specs=(VMEM, VMEM),
        scratch_shapes=[pltpu.VMEM((groups, 16, cols), BF16), pltpu.SemaphoreType.DMA],
        compiler_params=pltpu.CompilerParams(vmem_limit_bytes=32 * MIB),
        name="masks",
    )(*in_hbm(weights), modality, owner_ids)


def attend_kernel(given_ref, near_ref, bias_ref, out_ref):
    tok = given_ref.shape[0]
    mine = given_ref[:, HD:]
    tile = min(256, tok)

    def run(keys, values):
        for at in range(0, tok, tile):
            scores = dot_nt(given_ref[at : at + tile, :HD], keys) * (1.0 / math.sqrt(HD))
            scores = scores + bias_ref[at : at + tile, :].astype(F32)
            powered = jnp.exp(scores - jnp.max(scores, axis=1, keepdims=True))
            inverse = 1.0 / jnp.sum(powered, axis=1, keepdims=True)
            mixed = dot((powered * inverse).astype(BF16), values).astype(BF16)
            out_ref[0, at : at + tile, :] = mixed
            out_ref[1, at : at + tile, :] = mixed

    even = lax.axis_index("tp") % 2 == 0

    @pl.when(even)
    def _():
        run(mine, near_ref[...])

    @pl.when(jnp.logical_not(even))
    def _():
        run(near_ref[...], mine)


def attend(given, near, bias):
    tok = bias.shape[0]
    return pl.pallas_call(
        attend_kernel,
        out_shape=jax.ShapeDtypeStruct((2, tok, HD), BF16),
        in_specs=[VMEM] * 3,
        out_specs=VMEM,
        compiler_params=pltpu.CompilerParams(vmem_limit_bytes=24 * MIB),
        name="attend",
    )(given, near, bias)


def restore_kernel(back_ref, given_ref, out_ref):
    for core in range(2):
        out_ref[0, :, core * HD : (core + 1) * HD] = dot(back_ref[...], given_ref[core]).astype(BF16)


def restore(back, given):
    tok = back.shape[0]
    return pl.pallas_call(
        restore_kernel,
        out_shape=jax.ShapeDtypeStruct((1, tok, 2 * HD), BF16),
        in_specs=[VMEM, VMEM],
        out_specs=VMEM,
        compiler_params=pltpu.CompilerParams(vmem_limit_bytes=16 * MIB),
        name="restore",
    )(back, given)


def swap_all(value, axes):
    return lax.all_to_all(value, axes, split_axis=0, concat_axis=0, tiled=True)


def local(tokens, modality, doc_ids, owner_ids, norm_gain, query_weight, pair_weight):
    groups = lax.axis_size("grp")
    tok = tokens.shape[0]
    slots = tok // groups
    spread = pack(modality, owner_ids, doc_ids, query_weight, pair_weight, groups)
    weights = swap_all(spread, "grp")
    chosen = choose(modality, tokens)
    lifted = (chosen.astype(F32) * LIFT).astype(jnp.float16)
    gathered = lax.all_gather(lifted, "tp", axis=0)
    features = (gathered.astype(F32) * (1.0 / LIFT)).astype(BF16)
    keep, mine, give = project(normalize(features, norm_gain), weights)
    got = lax.ppermute(give, "tower", [(0, 1), (1, 0)])
    keep, later, owners = lax.optimization_barrier((keep, modality, owner_ids))
    sent = place(plan(later, owners, groups), keep, got, mine)
    sent, weights, later, owners = lax.optimization_barrier((sent, weights, later, owners))
    given = swap_all(sent.reshape(groups, slots, 2 * HD), "grp").reshape(tok, 2 * HD)
    bias, back = masks(weights, later, owners)
    near = lax.ppermute(given[:, HD:], "tp", [(t, t ^ 1) for t in range(lax.axis_size("tp"))])
    mixed = attend(given, near, bias)
    returned = swap_all(mixed.reshape(2 * groups, slots, HD), ("tower", "grp"))
    return restore(back, returned.reshape(2, tok, HD))


def solution(mesh):
    in_specs = (
        P("grp", "tp"),
        P("grp"),
        P("grp"),
        P("grp"),
        P("tower", None),
        P("tower", "grp", "tp"),
        P("tower", "grp", None),
    )
    out_specs = P("tower", "grp", "tp")
    return jax.shard_map(local, mesh=mesh, in_specs=in_specs, out_specs=out_specs, check_vma=False)
```

```python
import functools
import math

import jax
import jax.numpy as jnp
from jax import lax
from jax.experimental import pallas as pl
from jax.experimental.pallas import tpu as pltpu
from jax.sharding import PartitionSpec as P

HD = 128
EPS = 1e-05
MASKED = -1e30
LIFT = 64.0
MIB = 2**20
BF16, F32, I32 = jnp.bfloat16, jnp.float32, jnp.int32
VMEM = pl.BlockSpec(memory_space=pltpu.VMEM)
HBM = pl.BlockSpec(memory_space=pltpu.HBM)


def iota(shape, dim):
    return lax.broadcasted_iota(I32, shape, dim)


def ones_where(mask):
    return jnp.where(mask, 1.0, 0.0).astype(BF16)


def dot(a, b):
    return jnp.dot(a, b, preferred_element_type=F32)


def dot_nt(a, b):
    return lax.dot_general(a, b, (((1,), (1,)), ((), ())), preferred_element_type=F32)


def fold(parts):
    return functools.reduce(lambda a, b: a + b, parts)


def split_number(value):
    high = lax.shift_right_logical(value, 5)
    return high.astype(F32), (value - 32 * high).astype(F32)


def stack_rows(rows):
    shape = (8, rows[0].shape[1])
    at = iota(shape, 0)
    return fold(jnp.where(at == k, row, 0.0) for k, row in enumerate(rows)).astype(BF16)


def slots_of(modality, owner, groups):
    tok = owner.shape[1]
    slots = tok // groups
    match = iota((groups, tok), 0) == owner
    text = jnp.where(match & (modality == 0), 1.0, 0.0)
    image = jnp.where(match & (modality == 1), 1.0, 0.0)
    both = jnp.concatenate([text, image], axis=0)
    before = ones_where(iota((tok, tok), 0) < iota((tok, tok), 1))
    counts = dot(both.astype(BF16), before)
    in_owner = counts * both
    text_slot = jnp.sum(in_owner[:groups], axis=0, keepdims=True)
    image_slot = (slots - 1.0) - jnp.sum(in_owner[groups:], axis=0, keepdims=True)
    slot = jnp.where(modality == 1, image_slot, text_slot).astype(I32)
    text_rank = jnp.sum(counts[:groups], axis=0, keepdims=True)
    image_rank = jnp.sum(counts[groups:], axis=0, keepdims=True)
    rank = jnp.where(modality == 1, image_rank, text_rank).astype(I32)
    return owner * slots + slot, rank


def row_of(ref):
    return ref[...].reshape(1, ref.shape[0])


def in_hbm(*arrays):
    return tuple(pltpu.with_memory_space_constraint(a, pltpu.HBM) for a in arrays)


def pack_kernel(
    groups, modality_ref, owner_ref, doc_ref, token_ref, query_ref, pair_ref,
    chosen_ref, packed_ref, block, modality_own, owner_own, doc_own, token_own, sems,
):
    tok, half = token_ref.shape[0], chosen_ref.shape[0]
    rows, head_cols = query_ref.shape[1:]
    cols = packed_ref.shape[1]
    pair_heads = pair_ref.shape[2] // (2 * HD)
    column = lax.axis_index("tp") // (lax.axis_size("tp") // pair_heads) * 2 * HD
    sources = (
        (modality_ref, modality_own),
        (owner_ref, owner_own),
        (doc_ref, doc_own),
        (query_ref.at[0], block.at[pl.ds(0, rows), pl.ds(0, head_cols)]),
        (
            pair_ref.at[0, :, pl.ds(pl.multiple_of(column, HD), 2 * HD)],
            block.at[pl.ds(0, rows), pl.ds(head_cols, 2 * HD)],
        ),
        (token_ref, token_own),
    )
    loads = [
        pltpu.make_async_copy(source, target, sems.at[k])
        for k, (source, target) in enumerate(sources)
    ]
    for copy in loads:
        copy.start()
    for copy in loads[:3]:
        copy.wait()
    modality = row_of(modality_own)
    dest, own_rank = slots_of(modality, row_of(owner_own), groups)
    high, low = split_number(iota((1, tok), 1))
    facts = stack_rows([row_of(doc_own).astype(F32), high, low, modality.astype(F32)])
    table = dot_nt(facts, ones_where(iota((tok, tok), 0) == dest))
    if tok < 2 * cols:
        table = jnp.concatenate([table, jnp.zeros((8, 2 * cols - tok), F32)], axis=1)
    block[rows : rows + 16, :] = jnp.concatenate(
        [table[:, :cols], table[:, cols:]], axis=0
    ).astype(BF16)
    for copy in loads[3:5]:
        copy.wait()
    store = pltpu.make_async_copy(block, packed_ref, sems.at[len(loads)])
    store.start()
    own_rank = jnp.where(modality == lax.axis_index("tower"), own_rank, half)
    select = ones_where(iota((half, tok), 0) == own_rank)
    loads[5].wait()
    chosen_ref[...] = dot(select, token_own[...]).astype(BF16)
    store.wait()


def pack(modality, owner_ids, doc_ids, tokens, query_weight, pair_weight, groups):
    tok, slab = tokens.shape
    rows, head_cols = query_weight.shape[1:]
    cols = head_cols + 2 * HD
    return pl.pallas_call(
        functools.partial(pack_kernel, groups),
        out_shape=(
            jax.ShapeDtypeStruct((tok // 2, slab), BF16),
            pltpu.HBM((rows + 16, cols), BF16),
        ),
        in_specs=[HBM] * 6,
        out_specs=(VMEM, HBM),
        scratch_shapes=[
            pltpu.VMEM((rows + 16, cols), BF16),
            pltpu.VMEM((tok,), I32),
            pltpu.VMEM((tok,), I32),
            pltpu.VMEM((tok,), I32),
            pltpu.VMEM((tok, slab), BF16),
            pltpu.SemaphoreType.DMA((7,)),
        ],
        compiler_params=pltpu.CompilerParams(vmem_limit_bytes=24 * MIB),
        name="pack",
    )(*in_hbm(modality, owner_ids, doc_ids, tokens, query_weight, pair_weight))


def normalize_kernel(feature_ref, gain_ref, out_ref):
    count, half, slab = feature_ref.shape
    tile = 48 if half % 48 == 0 else 16

    @pl.loop(0, half // tile)
    def _(step):
        at = pl.ds(pl.multiple_of(step * tile, 16), tile)
        squares = jnp.zeros((tile, HD), F32)
        for k in range(count):
            values = feature_ref[k, at, :].astype(F32)
            squared = values * values
            squares += fold([squared[:, c : c + HD] for c in range(0, slab, HD)])
        mean = jnp.sum(squares, axis=1, keepdims=True) * (1.0 / (count * slab))
        inverse = lax.rsqrt(mean + EPS)
        for k in range(count):
            values = feature_ref[k, at, :].astype(F32) * inverse
            gain = gain_ref[:, k * slab : (k + 1) * slab]
            out_ref[k, at, :] = (values * gain).astype(BF16)


def normalize(features, gain):
    return pl.pallas_call(
        normalize_kernel,
        out_shape=jax.ShapeDtypeStruct(features.shape, BF16),
        in_specs=[VMEM, VMEM],
        out_specs=VMEM,
        compiler_params=pltpu.CompilerParams(vmem_limit_bytes=20 * MIB),
        name="normalize",
    )(features, gain)


def project_kernel(normed_ref, weight_ref, keep_ref, mine_ref, give_ref, rows, block, sems):
    count, _, slab = normed_ref.shape
    loads = []
    for k in range(count):
        loads.append(
            (
                pltpu.make_async_copy(normed_ref.at[k], rows.at[k], sems.at[2 * k]),
                pltpu.make_async_copy(
                    weight_ref.at[k, pl.ds(0, slab)], block.at[k], sems.at[2 * k + 1]
                ),
            )
        )
    for pair in loads:
        for copy in pair:
            copy.start()
    total = None
    together = 2
    for at in range(0, count, together):
        for pair in loads[at : at + together]:
            for copy in pair:
                copy.wait()
        term = fold([dot(rows[k], block[k]) for k in range(at, at + together)])
        total = term if total is None else total + term
    total = total.astype(BF16)
    pair = total[:, 2 * HD :]
    mine_ref[...] = pair
    give_ref[:, HD:] = pair
    text = lax.axis_index("tower") == 0

    @pl.when(text)
    def _():
        keep_ref[...] = total[:, :HD]
        give_ref[:, :HD] = total[:, HD : 2 * HD]

    @pl.when(jnp.logical_not(text))
    def _():
        keep_ref[...] = total[:, HD : 2 * HD]
        give_ref[:, :HD] = total[:, :HD]


def project(normed, weights):
    count, half, slab = normed.shape
    groups, rows, cols = weights.shape
    assert groups == count and rows == slab + 16 and cols == 4 * HD
    return pl.pallas_call(
        project_kernel,
        out_shape=(
            jax.ShapeDtypeStruct((half, HD), BF16),
            jax.ShapeDtypeStruct((half, 2 * HD), BF16),
            jax.ShapeDtypeStruct((half, 3 * HD), BF16),
        ),
        in_specs=[HBM, HBM],
        out_specs=(VMEM,) * 3,
        scratch_shapes=[
            pltpu.VMEM((count, half, slab), BF16),
            pltpu.VMEM((count, slab, cols), BF16),
            pltpu.SemaphoreType.DMA((2 * count,)),
        ],
        compiler_params=pltpu.CompilerParams(vmem_limit_bytes=32 * MIB),
        name="project",
    )(*in_hbm(normed, weights))


def plan_kernel(groups, modality_ref, owner_ref, place_ref):
    tok = place_ref.shape[0]
    half = tok // 2
    modality = row_of(modality_ref)
    dest, rank = slots_of(modality, row_of(owner_ref), groups)
    rank = jnp.where(modality == lax.axis_index("tower"), rank, half + rank)
    select = ones_where(iota((tok, tok), 0) == rank)
    high, low = split_number(dest)
    packed = dot_nt(stack_rows([high, low]), select)
    packed = (32.0 * packed[0:1] + packed[1:2]).astype(I32)
    place_ref[...] = ones_where(iota((tok, tok), 0) == packed)


def plan(modality, owner_ids, groups):
    tok = modality.shape[0]
    return pl.pallas_call(
        functools.partial(plan_kernel, groups),
        out_shape=jax.ShapeDtypeStruct((tok, tok), BF16),
        in_specs=[VMEM, VMEM],
        out_specs=VMEM,
        compiler_params=pltpu.CompilerParams(vmem_limit_bytes=24 * MIB),
        name="plan",
    )(modality, owner_ids)


def place_kernel(place_ref, keep_ref, got_ref, mine_ref, out_ref):
    half = keep_ref.shape[0]
    own, other = place_ref[:, :half], place_ref[:, half:]
    out_ref[:, :HD] = (dot(own, keep_ref[...]) + dot(other, got_ref[:, :HD])).astype(BF16)
    out_ref[:, HD:] = (dot(own, mine_ref[...]) + dot(other, got_ref[:, HD:])).astype(BF16)


def place(where, keep, got, mine):
    tok = where.shape[0]
    return pl.pallas_call(
        place_kernel,
        out_shape=jax.ShapeDtypeStruct((tok, 3 * HD), BF16),
        in_specs=[VMEM] * 4,
        out_specs=VMEM,
        compiler_params=pltpu.CompilerParams(vmem_limit_bytes=16 * MIB),
        name="place",
    )(where, keep, got, mine)


def mask_kernel(note_ref, modality_ref, owner_ref, bias_ref, back_ref, notes, sem):
    groups, rows, cols = note_ref.shape
    tok = bias_ref.shape[0]
    slots = tok // groups
    copy = pltpu.make_async_copy(note_ref.at[:, pl.ds(rows - 16, 16)], notes, sem)
    copy.start()
    modality = row_of(modality_ref)
    dest, _ = slots_of(modality, row_of(owner_ref), groups)
    same = ones_where(iota((tok, tok), 0) == iota((tok, tok), 1))
    high, low = split_number(dest)
    mine = jnp.where(modality == lax.axis_index("tower"), 1.0, 0.0)
    back = dot_nt(same, stack_rows([high, low, mine]))
    dest = (32.0 * back[:, 0:1] + back[:, 1:2]).astype(I32)
    dest = jnp.where(back[:, 2:3] > 0.5, dest, -1)
    back_ref[...] = ones_where(iota((tok, tok), 1) == dest)

    copy.wait()
    group = lax.axis_index("grp")
    seen = notes[...].astype(F32)
    facts = jnp.concatenate([seen[:, :8], seen[:, 8:]], axis=2)[:, :, :tok]
    facts = facts.reshape(groups * 8, tok).astype(BF16)

    def part(index):
        return jnp.floor((index.astype(F32) + 0.5) * (1.0 / slots))

    column = iota((1, tok), 1)
    from_group = part(column)
    slot = column - slots * from_group.astype(I32)
    take = ones_where(iota((tok, tok), 0) == group * slots + slot)
    seen = dot(facts, take).reshape(groups, 8, tok)
    at = iota((groups, 8, tok), 0)
    row = jnp.sum(jnp.where(at == from_group.astype(I32)[None], seen, 0.0), axis=0)
    turned = dot_nt(same, row.astype(BF16))
    row_place = tok * from_group + 32.0 * row[1:2] + row[2:3]
    turned_place = tok * part(iota((tok, 1), 0)) + 32.0 * turned[:, 1:2] + turned[:, 2:3]
    after = (row_place <= turned_place) | (row[3:4] * turned[:, 3:4] > 0.5)
    allowed = (row[0:1] == turned[:, 0:1]) & after
    bias_ref[...] = jnp.where(allowed, 0.0, MASKED).astype(BF16)


def masks(weights, modality, owner_ids):
    tok = modality.shape[0]
    groups, _, cols = weights.shape
    return pl.pallas_call(
        mask_kernel,
        out_shape=(
            jax.ShapeDtypeStruct((tok, tok), BF16),
            jax.ShapeDtypeStruct((tok, tok), BF16),
        ),
        in_specs=[HBM, VMEM, VMEM],
        out_specs=(VMEM, VMEM),
        scratch_shapes=[pltpu.VMEM((groups, 16, cols), BF16), pltpu.SemaphoreType.DMA],
        compiler_params=pltpu.CompilerParams(vmem_limit_bytes=32 * MIB),
        name="masks",
    )(*in_hbm(weights), modality, owner_ids)


def attend_kernel(given_ref, bias_ref, out_ref):
    tok = given_ref.shape[0]
    keys, values = given_ref[:, HD : 2 * HD], given_ref[:, 2 * HD :]
    tile = min(256, tok)
    for at in range(0, tok, tile):
        scores = dot_nt(given_ref[at : at + tile, :HD], keys) * (1.0 / math.sqrt(HD))
        scores = scores + bias_ref[at : at + tile, :].astype(F32)
        powered = jnp.exp(scores - jnp.max(scores, axis=1, keepdims=True))
        inverse = 1.0 / jnp.sum(powered, axis=1, keepdims=True)
        mixed = dot((powered * inverse).astype(BF16), values).astype(BF16)
        out_ref[0, at : at + tile, :] = mixed
        out_ref[1, at : at + tile, :] = mixed


def attend(given, bias):
    tok = bias.shape[0]
    return pl.pallas_call(
        attend_kernel,
        out_shape=jax.ShapeDtypeStruct((2, tok, HD), BF16),
        in_specs=[VMEM, VMEM],
        out_specs=VMEM,
        compiler_params=pltpu.CompilerParams(vmem_limit_bytes=24 * MIB),
        name="attend",
    )(given, bias)


def restore_kernel(back_ref, given_ref, out_ref):
    for core in range(2):
        out_ref[0, :, core * HD : (core + 1) * HD] = dot(back_ref[...], given_ref[core]).astype(BF16)


def restore(back, given):
    tok = back.shape[0]
    return pl.pallas_call(
        restore_kernel,
        out_shape=jax.ShapeDtypeStruct((1, tok, 2 * HD), BF16),
        in_specs=[VMEM, VMEM],
        out_specs=VMEM,
        compiler_params=pltpu.CompilerParams(vmem_limit_bytes=16 * MIB),
        name="restore",
    )(back, given)


def swap_all(value, axes):
    return lax.all_to_all(value, axes, split_axis=0, concat_axis=0, tiled=True)


def local(tokens, modality, doc_ids, owner_ids, norm_gain, query_weight, pair_weight):
    groups = lax.axis_size("grp")
    tok = tokens.shape[0]
    slots = tok // groups
    chosen, packed = pack(
        modality, owner_ids, doc_ids, tokens, query_weight, pair_weight, groups
    )
    weights = lax.all_gather(packed, "grp", axis=0)
    lifted = (chosen.astype(F32) * LIFT).astype(jnp.float16)
    gathered = lax.all_gather(lifted, "tp", axis=0)
    features = (gathered.astype(F32) * (1.0 / LIFT)).astype(BF16)
    normed, later, owners = lax.optimization_barrier(
        (normalize(features, norm_gain), modality, owner_ids)
    )
    where = plan(later, owners, groups)
    keep, mine, give = project(normed, weights)
    got = lax.ppermute(give, "tower", [(0, 1), (1, 0)])
    sent = place(where, keep, got, mine)
    sent, weights, later, owners = lax.optimization_barrier((sent, weights, later, owners))
    given = swap_all(sent.reshape(groups, slots, 3 * HD), "grp").reshape(tok, 3 * HD)
    bias, back = masks(weights, later, owners)
    mixed = attend(given, bias)
    returned = swap_all(mixed.reshape(2 * groups, slots, HD), ("tower", "grp"))
    return restore(back, returned.reshape(2, tok, HD))


def solution(mesh):
    in_specs = (
        P("grp", "tp"),
        P("grp"),
        P("grp"),
        P("grp"),
        P("tower", None),
        P("tower", "grp", "tp"),
        P("tower", "grp", None),
    )
    out_specs = P("tower", "grp", "tp")
    return jax.shard_map(local, mesh=mesh, in_specs=in_specs, out_specs=out_specs, check_vma=False)
```

```python
import functools
import math

import jax
import jax.numpy as jnp
from jax import lax
from jax.experimental import pallas as pl
from jax.experimental.pallas import tpu as pltpu
from jax.sharding import PartitionSpec as P

HD = 128
EPS = 1e-05
MASKED = -1e30
LIFT = 64.0
MIB = 2**20
BF16, F32, I32 = jnp.bfloat16, jnp.float32, jnp.int32
VMEM = pl.BlockSpec(memory_space=pltpu.VMEM)
HBM = pl.BlockSpec(memory_space=pltpu.HBM)


def iota(shape, dim):
    return lax.broadcasted_iota(I32, shape, dim)


def ones_where(mask):
    return jnp.where(mask, 1.0, 0.0).astype(BF16)


def dot(a, b):
    return jnp.dot(a, b, preferred_element_type=F32)


def dot_nt(a, b):
    return lax.dot_general(a, b, (((1,), (1,)), ((), ())), preferred_element_type=F32)


def fold(parts):
    return functools.reduce(lambda a, b: a + b, parts)


def split_number(value):
    high = lax.shift_right_logical(value, 5)
    return high.astype(F32), (value - 32 * high).astype(F32)


def stack_rows(rows):
    shape = (8, rows[0].shape[1])
    at = iota(shape, 0)
    return fold(jnp.where(at == k, row, 0.0) for k, row in enumerate(rows)).astype(BF16)


def slots_of(modality, owner, groups):
    tok = owner.shape[1]
    slots = tok // groups
    match = iota((groups, tok), 0) == owner
    text = jnp.where(match & (modality == 0), 1.0, 0.0)
    image = jnp.where(match & (modality == 1), 1.0, 0.0)
    both = jnp.concatenate([text, image], axis=0)
    before = ones_where(iota((tok, tok), 0) < iota((tok, tok), 1))
    counts = dot(both.astype(BF16), before)
    in_owner = counts * both
    text_slot = jnp.sum(in_owner[:groups], axis=0, keepdims=True)
    image_slot = (slots - 1.0) - jnp.sum(in_owner[groups:], axis=0, keepdims=True)
    slot = jnp.where(modality == 1, image_slot, text_slot).astype(I32)
    text_rank = jnp.sum(counts[:groups], axis=0, keepdims=True)
    image_rank = jnp.sum(counts[groups:], axis=0, keepdims=True)
    rank = jnp.where(modality == 1, image_rank, text_rank).astype(I32)
    return owner * slots + slot, rank


def row_of(ref):
    return ref[...].reshape(1, ref.shape[0])


def in_hbm(*arrays):
    return tuple(pltpu.with_memory_space_constraint(a, pltpu.HBM) for a in arrays)


def pack_kernel(
    groups, modality_ref, owner_ref, doc_ref, token_ref, query_ref, pair_ref,
    chosen_ref, packed_ref, block, modality_own, owner_own, doc_own, token_own, sems,
):
    tok, half = token_ref.shape[0], chosen_ref.shape[0]
    rows, head_cols = query_ref.shape[1:]
    cols = packed_ref.shape[1]
    pair_heads = pair_ref.shape[2] // (2 * HD)
    column = lax.axis_index("tp") // (lax.axis_size("tp") // pair_heads) * 2 * HD
    sources = (
        (modality_ref, modality_own),
        (owner_ref, owner_own),
        (doc_ref, doc_own),
        (query_ref.at[0], block.at[pl.ds(0, rows), pl.ds(0, head_cols)]),
        (
            pair_ref.at[0, :, pl.ds(pl.multiple_of(column, HD), 2 * HD)],
            block.at[pl.ds(0, rows), pl.ds(head_cols, 2 * HD)],
        ),
        (token_ref, token_own),
    )
    loads = [
        pltpu.make_async_copy(source, target, sems.at[k])
        for k, (source, target) in enumerate(sources)
    ]
    for copy in loads:
        copy.start()
    for copy in loads[:3]:
        copy.wait()
    modality = row_of(modality_own)
    dest, own_rank = slots_of(modality, row_of(owner_own), groups)
    high, low = split_number(iota((1, tok), 1))
    facts = stack_rows([row_of(doc_own).astype(F32), high, low, modality.astype(F32)])
    table = dot_nt(facts, ones_where(iota((tok, tok), 0) == dest))
    if tok < 2 * cols:
        table = jnp.concatenate([table, jnp.zeros((8, 2 * cols - tok), F32)], axis=1)
    block[rows : rows + 16, :] = jnp.concatenate(
        [table[:, :cols], table[:, cols:]], axis=0
    ).astype(BF16)
    for copy in loads[3:5]:
        copy.wait()
    store = pltpu.make_async_copy(block, packed_ref, sems.at[len(loads)])
    store.start()
    own_rank = jnp.where(modality == lax.axis_index("tower"), own_rank, half)
    select = ones_where(iota((half, tok), 0) == own_rank)
    loads[5].wait()
    chosen_ref[...] = dot(select, token_own[...]).astype(BF16)
    store.wait()


def pack(modality, owner_ids, doc_ids, tokens, query_weight, pair_weight, groups):
    tok, slab = tokens.shape
    rows, head_cols = query_weight.shape[1:]
    cols = head_cols + 2 * HD
    return pl.pallas_call(
        functools.partial(pack_kernel, groups),
        out_shape=(
            jax.ShapeDtypeStruct((tok // 2, slab), BF16),
            pltpu.HBM((rows + 16, cols), BF16),
        ),
        in_specs=[HBM] * 6,
        out_specs=(VMEM, HBM),
        scratch_shapes=[
            pltpu.VMEM((rows + 16, cols), BF16),
            pltpu.VMEM((tok,), I32),
            pltpu.VMEM((tok,), I32),
            pltpu.VMEM((tok,), I32),
            pltpu.VMEM((tok, slab), BF16),
            pltpu.SemaphoreType.DMA((7,)),
        ],
        compiler_params=pltpu.CompilerParams(vmem_limit_bytes=24 * MIB),
        name="pack",
    )(*in_hbm(modality, owner_ids, doc_ids, tokens, query_weight, pair_weight))


def normalize_kernel(feature_ref, gain_ref, early_ref, late_ref):
    count, half, slab = feature_ref.shape
    early = early_ref.shape[0]
    tile = 48 if half % 48 == 0 else 16

    @pl.loop(0, half // tile)
    def _(step):
        at = pl.ds(pl.multiple_of(step * tile, 16), tile)
        squares = jnp.zeros((tile, HD), F32)
        for k in range(count):
            values = feature_ref[k, at, :].astype(F32)
            squared = values * values
            squares += fold([squared[:, c : c + HD] for c in range(0, slab, HD)])
        mean = jnp.sum(squares, axis=1, keepdims=True) * (1.0 / (count * slab))
        inverse = lax.rsqrt(mean + EPS)
        for k in range(count):
            values = feature_ref[k, at, :].astype(F32) * inverse
            gain = gain_ref[:, k * slab : (k + 1) * slab]
            normed = (values * gain).astype(BF16)
            if k < early:
                early_ref[k, at, :] = normed
            else:
                late_ref[k - early, at, :] = normed


def normalize(features, gain):
    count, half, slab = features.shape
    early = count // 2
    return pl.pallas_call(
        normalize_kernel,
        out_shape=(
            jax.ShapeDtypeStruct((early, half, slab), BF16),
            jax.ShapeDtypeStruct((count - early, half, slab), BF16),
        ),
        in_specs=[VMEM, VMEM],
        out_specs=(VMEM, VMEM),
        compiler_params=pltpu.CompilerParams(vmem_limit_bytes=20 * MIB),
        name="normalize",
    )(features, gain)


def project_kernel(
    early_ref, late_ref, weight_ref, keep_ref, mine_ref, give_ref, rows, block, sems
):
    early, _, slab = early_ref.shape
    count = early + late_ref.shape[0]
    weights = [
        pltpu.make_async_copy(weight_ref.at[k, pl.ds(0, slab)], block.at[k], sems.at[k])
        for k in range(count)
    ]
    lates = [
        pltpu.make_async_copy(late_ref.at[k], rows.at[k], sems.at[count + k])
        for k in range(count - early)
    ]
    for k in range(count):
        weights[k].start()
        if k >= early:
            lates[k - early].start()
    total = None
    together = 1
    for at in range(0, count, together):
        terms = []
        for k in range(at, at + together):
            weights[k].wait()
            if k >= early:
                lates[k - early].wait()
            terms.append(dot(early_ref[k] if k < early else rows[k - early], block[k]))
        term = fold(terms)
        total = term if total is None else total + term
    total = total.astype(BF16)
    pair = total[:, 2 * HD :]
    mine_ref[...] = pair
    give_ref[:, HD:] = pair
    text = lax.axis_index("tower") == 0

    @pl.when(text)
    def _():
        keep_ref[...] = total[:, :HD]
        give_ref[:, :HD] = total[:, HD : 2 * HD]

    @pl.when(jnp.logical_not(text))
    def _():
        keep_ref[...] = total[:, HD : 2 * HD]
        give_ref[:, :HD] = total[:, :HD]


def project(normed, weights):
    early, late = normed
    _, half, slab = early.shape
    groups, rows, cols = weights.shape
    assert groups == len(early) + len(late) and rows == slab + 16 and cols == 4 * HD
    return pl.pallas_call(
        project_kernel,
        out_shape=(
            jax.ShapeDtypeStruct((half, HD), BF16),
            jax.ShapeDtypeStruct((half, 2 * HD), BF16),
            jax.ShapeDtypeStruct((half, 3 * HD), BF16),
        ),
        in_specs=[VMEM, HBM, HBM],
        out_specs=(VMEM,) * 3,
        scratch_shapes=[
            pltpu.VMEM(late.shape, BF16),
            pltpu.VMEM((groups, slab, cols), BF16),
            pltpu.SemaphoreType.DMA((groups + len(late),)),
        ],
        compiler_params=pltpu.CompilerParams(vmem_limit_bytes=24 * MIB),
        name="project",
    )(early, *in_hbm(late, weights))


def plan_kernel(groups, modality_ref, owner_ref, place_ref):
    tok = place_ref.shape[0]
    half = tok // 2
    modality = row_of(modality_ref)
    dest, rank = slots_of(modality, row_of(owner_ref), groups)
    rank = jnp.where(modality == lax.axis_index("tower"), rank, half + rank)
    select = ones_where(iota((tok, tok), 0) == rank)
    high, low = split_number(dest)
    packed = dot_nt(stack_rows([high, low]), select)
    packed = (32.0 * packed[0:1] + packed[1:2]).astype(I32)
    place_ref[...] = ones_where(iota((tok, tok), 0) == packed)


def plan(modality, owner_ids, groups):
    tok = modality.shape[0]
    return pl.pallas_call(
        functools.partial(plan_kernel, groups),
        out_shape=jax.ShapeDtypeStruct((tok, tok), BF16),
        in_specs=[VMEM, VMEM],
        out_specs=VMEM,
        compiler_params=pltpu.CompilerParams(vmem_limit_bytes=24 * MIB),
        name="plan",
    )(modality, owner_ids)


def place_kernel(place_ref, keep_ref, got_ref, mine_ref, out_ref):
    own = jnp.concatenate([keep_ref[...], mine_ref[...]], axis=1)
    rows = jnp.concatenate([own, got_ref[...]], axis=0)
    out_ref[...] = dot(place_ref[...], rows).astype(BF16)


def place(where, keep, got, mine):
    tok = where.shape[0]
    return pl.pallas_call(
        place_kernel,
        out_shape=jax.ShapeDtypeStruct((tok, 3 * HD), BF16),
        in_specs=[VMEM] * 4,
        out_specs=VMEM,
        compiler_params=pltpu.CompilerParams(vmem_limit_bytes=16 * MIB),
        name="place",
    )(where, keep, got, mine)


def mask_kernel(note_ref, modality_ref, owner_ref, bias_ref, back_ref, notes, sem):
    groups, rows, cols = note_ref.shape
    tok = bias_ref.shape[0]
    slots = tok // groups
    copy = pltpu.make_async_copy(note_ref.at[:, pl.ds(rows - 16, 16)], notes, sem)
    copy.start()
    modality = row_of(modality_ref)
    dest, _ = slots_of(modality, row_of(owner_ref), groups)
    same = ones_where(iota((tok, tok), 0) == iota((tok, tok), 1))
    high, low = split_number(dest)
    mine = jnp.where(modality == lax.axis_index("tower"), 1.0, 0.0)
    back = dot_nt(same, stack_rows([high, low, mine]))
    dest = (32.0 * back[:, 0:1] + back[:, 1:2]).astype(I32)
    dest = jnp.where(back[:, 2:3] > 0.5, dest, -1)
    back_ref[...] = ones_where(iota((tok, tok), 1) == dest)

    copy.wait()
    group = lax.axis_index("grp")
    seen = notes[...].astype(F32)
    facts = jnp.concatenate([seen[:, :8], seen[:, 8:]], axis=2)[:, :, :tok]
    facts = facts.reshape(groups * 8, tok).astype(BF16)

    def part(index):
        return jnp.floor((index.astype(F32) + 0.5) * (1.0 / slots))

    column = iota((1, tok), 1)
    from_group = part(column)
    slot = column - slots * from_group.astype(I32)
    take = ones_where(iota((tok, tok), 0) == group * slots + slot)
    seen = dot(facts, take).reshape(groups, 8, tok)
    at = iota((groups, 8, tok), 0)
    row = jnp.sum(jnp.where(at == from_group.astype(I32)[None], seen, 0.0), axis=0)
    turned = dot_nt(same, row.astype(BF16))
    row_place = tok * from_group + 32.0 * row[1:2] + row[2:3]
    turned_place = tok * part(iota((tok, 1), 0)) + 32.0 * turned[:, 1:2] + turned[:, 2:3]
    after = (row_place <= turned_place) | (row[3:4] * turned[:, 3:4] > 0.5)
    allowed = (row[0:1] == turned[:, 0:1]) & after
    bias_ref[...] = jnp.where(allowed, 0.0, MASKED).astype(BF16)


def masks(weights, modality, owner_ids):
    tok = modality.shape[0]
    groups, _, cols = weights.shape
    return pl.pallas_call(
        mask_kernel,
        out_shape=(
            jax.ShapeDtypeStruct((tok, tok), BF16),
            jax.ShapeDtypeStruct((tok, tok), BF16),
        ),
        in_specs=[HBM, VMEM, VMEM],
        out_specs=(VMEM, VMEM),
        scratch_shapes=[pltpu.VMEM((groups, 16, cols), BF16), pltpu.SemaphoreType.DMA],
        compiler_params=pltpu.CompilerParams(vmem_limit_bytes=32 * MIB),
        name="masks",
    )(*in_hbm(weights), modality, owner_ids)


def attend_kernel(given_ref, bias_ref, out_ref):
    tok = given_ref.shape[0]
    keys, values = given_ref[:, HD : 2 * HD], given_ref[:, 2 * HD :]
    tile = min(256, tok)
    for at in range(0, tok, tile):
        scores = dot_nt(given_ref[at : at + tile, :HD], keys) * (1.0 / math.sqrt(HD))
        scores = scores + bias_ref[at : at + tile, :].astype(F32)
        powered = jnp.exp(scores - jnp.max(scores, axis=1, keepdims=True))
        inverse = 1.0 / jnp.sum(powered, axis=1, keepdims=True)
        mixed = dot((powered * inverse).astype(BF16), values).astype(BF16)
        out_ref[0, at : at + tile, :] = mixed
        out_ref[1, at : at + tile, :] = mixed


def attend(given, bias):
    tok = bias.shape[0]
    return pl.pallas_call(
        attend_kernel,
        out_shape=jax.ShapeDtypeStruct((2, tok, HD), BF16),
        in_specs=[VMEM, VMEM],
        out_specs=VMEM,
        compiler_params=pltpu.CompilerParams(vmem_limit_bytes=24 * MIB),
        name="attend",
    )(given, bias)


def restore_kernel(back_ref, given_ref, out_ref):
    both = jnp.concatenate([given_ref[0], given_ref[1]], axis=1)
    out_ref[0] = dot(back_ref[...], both).astype(BF16)


def restore(back, given):
    tok = back.shape[0]
    return pl.pallas_call(
        restore_kernel,
        out_shape=jax.ShapeDtypeStruct((1, tok, 2 * HD), BF16),
        in_specs=[VMEM, VMEM],
        out_specs=VMEM,
        compiler_params=pltpu.CompilerParams(vmem_limit_bytes=16 * MIB),
        name="restore",
    )(back, given)


def swap_all(value, axes):
    return lax.all_to_all(value, axes, split_axis=0, concat_axis=0, tiled=True)


def local(tokens, modality, doc_ids, owner_ids, norm_gain, query_weight, pair_weight):
    groups = lax.axis_size("grp")
    tok = tokens.shape[0]
    slots = tok // groups
    chosen, packed = pack(
        modality, owner_ids, doc_ids, tokens, query_weight, pair_weight, groups
    )
    weights = lax.all_gather(packed, "grp", axis=0)
    lifted = (chosen.astype(F32) * LIFT).astype(jnp.float16)
    gathered = lax.all_gather(lifted, "tp", axis=0)
    features = (gathered.astype(F32) * (1.0 / LIFT)).astype(BF16)
    keep, mine, give = project(normalize(features, norm_gain), weights)
    got = lax.ppermute(give, "tower", [(0, 1), (1, 0)])
    keep, later, owners = lax.optimization_barrier((keep, modality, owner_ids))
    sent = place(plan(later, owners, groups), keep, got, mine)
    sent, weights, later, owners = lax.optimization_barrier((sent, weights, later, owners))
    given = swap_all(sent.reshape(groups, slots, 3 * HD), "grp").reshape(tok, 3 * HD)
    bias, back = masks(weights, later, owners)
    mixed = attend(given, bias)
    returned = swap_all(mixed.reshape(2 * groups, slots, HD), ("tower", "grp"))
    return restore(back, returned.reshape(2, tok, HD))


def solution(mesh):
    in_specs = (
        P("grp", "tp"),
        P("grp"),
        P("grp"),
        P("grp"),
        P("tower", None),
        P("tower", "grp", "tp"),
        P("tower", "grp", None),
    )
    out_specs = P("tower", "grp", "tp")
    return jax.shard_map(local, mesh=mesh, in_specs=in_specs, out_specs=out_specs, check_vma=False)
```

```python
import functools
import math

import jax
import jax.numpy as jnp
from jax import lax
from jax.experimental import pallas as pl
from jax.experimental.pallas import tpu as pltpu
from jax.sharding import PartitionSpec as P

HD = 128
EPS = 1e-05
MASKED = -1e30
LIFT = 64.0
MIB = 2**20
BF16, F32, I32 = jnp.bfloat16, jnp.float32, jnp.int32
VMEM = pl.BlockSpec(memory_space=pltpu.VMEM)
HBM = pl.BlockSpec(memory_space=pltpu.HBM)


def iota(shape, dim):
    return lax.broadcasted_iota(I32, shape, dim)


def ones_where(mask):
    return jnp.where(mask, 1.0, 0.0).astype(BF16)


def dot(a, b):
    return jnp.dot(a, b, preferred_element_type=F32)


def dot_nt(a, b):
    return lax.dot_general(a, b, (((1,), (1,)), ((), ())), preferred_element_type=F32)


def fold(parts):
    return functools.reduce(lambda a, b: a + b, parts)


def split_number(value):
    high = lax.shift_right_logical(value, 5)
    return high.astype(F32), (value - 32 * high).astype(F32)


def stack_rows(rows):
    shape = (8, rows[0].shape[1])
    at = iota(shape, 0)
    return fold(jnp.where(at == k, row, 0.0) for k, row in enumerate(rows)).astype(BF16)


def slots_of(modality, owner, groups):
    tok = owner.shape[1]
    slots = tok // groups
    match = iota((groups, tok), 0) == owner
    text = jnp.where(match & (modality == 0), 1.0, 0.0)
    image = jnp.where(match & (modality == 1), 1.0, 0.0)
    both = jnp.concatenate([text, image], axis=0)
    before = ones_where(iota((tok, tok), 0) < iota((tok, tok), 1))
    counts = dot(both.astype(BF16), before)
    in_owner = counts * both
    text_slot = jnp.sum(in_owner[:groups], axis=0, keepdims=True)
    image_slot = (slots - 1.0) - jnp.sum(in_owner[groups:], axis=0, keepdims=True)
    slot = jnp.where(modality == 1, image_slot, text_slot).astype(I32)
    text_rank = jnp.sum(counts[:groups], axis=0, keepdims=True)
    image_rank = jnp.sum(counts[groups:], axis=0, keepdims=True)
    rank = jnp.where(modality == 1, image_rank, text_rank).astype(I32)
    return owner * slots + slot, rank


def row_of(ref):
    return ref[...].reshape(1, ref.shape[0])


def in_hbm(*arrays):
    return tuple(pltpu.with_memory_space_constraint(a, pltpu.HBM) for a in arrays)


def pack_kernel(
    groups, modality_ref, owner_ref, doc_ref, token_ref, query_ref, pair_ref,
    chosen_ref, packed_ref, block, modality_own, owner_own, doc_own, token_own, sems,
):
    tok, half = token_ref.shape[0], chosen_ref.shape[0]
    rows, head_cols = query_ref.shape[1:]
    cols = packed_ref.shape[1]
    pair_heads = pair_ref.shape[2] // (2 * HD)
    column = lax.axis_index("tp") // (lax.axis_size("tp") // pair_heads) * 2 * HD
    sources = (
        (modality_ref, modality_own),
        (owner_ref, owner_own),
        (doc_ref, doc_own),
        (query_ref.at[0], block.at[pl.ds(0, rows), pl.ds(0, head_cols)]),
        (
            pair_ref.at[0, :, pl.ds(pl.multiple_of(column, HD), 2 * HD)],
            block.at[pl.ds(0, rows), pl.ds(head_cols, 2 * HD)],
        ),
        (token_ref, token_own),
    )
    loads = [
        pltpu.make_async_copy(source, target, sems.at[k])
        for k, (source, target) in enumerate(sources)
    ]
    for copy in loads:
        copy.start()
    for copy in loads[:3]:
        copy.wait()
    modality = row_of(modality_own)
    dest, own_rank = slots_of(modality, row_of(owner_own), groups)
    high, low = split_number(iota((1, tok), 1))
    facts = stack_rows([row_of(doc_own).astype(F32), high, low, modality.astype(F32)])
    table = dot_nt(facts, ones_where(iota((tok, tok), 0) == dest))
    if tok < 2 * cols:
        table = jnp.concatenate([table, jnp.zeros((8, 2 * cols - tok), F32)], axis=1)
    block[rows : rows + 16, :] = jnp.concatenate(
        [table[:, :cols], table[:, cols:]], axis=0
    ).astype(BF16)
    for copy in loads[3:5]:
        copy.wait()
    store = pltpu.make_async_copy(block, packed_ref, sems.at[len(loads)])
    store.start()
    own_rank = jnp.where(modality == lax.axis_index("tower"), own_rank, half)
    select = ones_where(iota((half, tok), 0) == own_rank)
    loads[5].wait()
    chosen_ref[...] = dot(select, token_own[...]).astype(BF16)
    store.wait()


def pack(modality, owner_ids, doc_ids, tokens, query_weight, pair_weight, groups):
    tok, slab = tokens.shape
    rows, head_cols = query_weight.shape[1:]
    cols = head_cols + 2 * HD
    return pl.pallas_call(
        functools.partial(pack_kernel, groups),
        out_shape=(
            jax.ShapeDtypeStruct((tok // 2, slab), BF16),
            pltpu.HBM((rows + 16, cols), BF16),
        ),
        in_specs=[HBM] * 6,
        out_specs=(VMEM, HBM),
        scratch_shapes=[
            pltpu.VMEM((rows + 16, cols), BF16),
            pltpu.VMEM((tok,), I32),
            pltpu.VMEM((tok,), I32),
            pltpu.VMEM((tok,), I32),
            pltpu.VMEM((tok, slab), BF16),
            pltpu.SemaphoreType.DMA((7,)),
        ],
        compiler_params=pltpu.CompilerParams(vmem_limit_bytes=24 * MIB),
        name="pack",
    )(*in_hbm(modality, owner_ids, doc_ids, tokens, query_weight, pair_weight))


def normalize_kernel(feature_ref, gain_ref, early_ref, late_ref):
    count, half, slab = feature_ref.shape
    early = early_ref.shape[0]
    tile = 48 if half % 48 == 0 else 16

    @pl.loop(0, half // tile)
    def _(step):
        at = pl.ds(pl.multiple_of(step * tile, 16), tile)
        squares = jnp.zeros((tile, HD), F32)
        for k in range(count):
            values = feature_ref[k, at, :].astype(F32)
            squared = values * values
            squares += fold([squared[:, c : c + HD] for c in range(0, slab, HD)])
        mean = jnp.sum(squares, axis=1, keepdims=True) * (1.0 / (count * slab))
        inverse = lax.rsqrt(mean + EPS)
        for k in range(count):
            values = feature_ref[k, at, :].astype(F32) * inverse
            gain = gain_ref[:, k * slab : (k + 1) * slab]
            normed = (values * gain).astype(BF16)
            if k < early:
                early_ref[k, at, :] = normed
            else:
                late_ref[k - early, at, :] = normed


def normalize(features, gain):
    count, half, slab = features.shape
    early = count // 2
    return pl.pallas_call(
        normalize_kernel,
        out_shape=(
            jax.ShapeDtypeStruct((early, half, slab), BF16),
            jax.ShapeDtypeStruct((count - early, half, slab), BF16),
        ),
        in_specs=[VMEM, VMEM],
        out_specs=(VMEM, VMEM),
        compiler_params=pltpu.CompilerParams(vmem_limit_bytes=20 * MIB),
        name="normalize",
    )(features, gain)


def project_kernel(
    early_ref, late_ref, weight_ref, keep_ref, mine_ref, give_ref, rows, block, sems
):
    early, _, slab = early_ref.shape
    count = early + late_ref.shape[0]
    weights = [
        pltpu.make_async_copy(weight_ref.at[k, pl.ds(0, slab)], block.at[k], sems.at[k])
        for k in range(count)
    ]
    lates = [
        pltpu.make_async_copy(late_ref.at[k], rows.at[k], sems.at[count + k])
        for k in range(count - early)
    ]
    for k in range(count):
        weights[k].start()
        if k >= early:
            lates[k - early].start()
    total = None
    together = 1
    for at in range(0, count, together):
        terms = []
        for k in range(at, at + together):
            weights[k].wait()
            if k >= early:
                lates[k - early].wait()
            terms.append(dot(early_ref[k] if k < early else rows[k - early], block[k]))
        term = fold(terms)
        total = term if total is None else total + term
    total = total.astype(BF16)
    pair = total[:, 2 * HD :]
    mine_ref[...] = pair
    give_ref[:, HD:] = pair
    text = lax.axis_index("tower") == 0

    @pl.when(text)
    def _():
        keep_ref[...] = total[:, :HD]
        give_ref[:, :HD] = total[:, HD : 2 * HD]

    @pl.when(jnp.logical_not(text))
    def _():
        keep_ref[...] = total[:, HD : 2 * HD]
        give_ref[:, :HD] = total[:, :HD]


def project(normed, weights):
    early, late = normed
    _, half, slab = early.shape
    groups, rows, cols = weights.shape
    assert groups == len(early) + len(late) and rows == slab + 16 and cols == 4 * HD
    return pl.pallas_call(
        project_kernel,
        out_shape=(
            jax.ShapeDtypeStruct((half, HD), BF16),
            jax.ShapeDtypeStruct((half, 2 * HD), BF16),
            jax.ShapeDtypeStruct((half, 3 * HD), BF16),
        ),
        in_specs=[VMEM, HBM, HBM],
        out_specs=(VMEM,) * 3,
        scratch_shapes=[
            pltpu.VMEM(late.shape, BF16),
            pltpu.VMEM((groups, slab, cols), BF16),
            pltpu.SemaphoreType.DMA((groups + len(late),)),
        ],
        compiler_params=pltpu.CompilerParams(vmem_limit_bytes=24 * MIB),
        name="project",
    )(early, *in_hbm(late, weights))


def plan_kernel(groups, modality_ref, owner_ref, place_ref):
    tok = place_ref.shape[0]
    half = tok // 2
    modality = row_of(modality_ref)
    dest, rank = slots_of(modality, row_of(owner_ref), groups)
    rank = jnp.where(modality == lax.axis_index("tower"), rank, half + rank)
    select = ones_where(iota((tok, tok), 0) == rank)
    high, low = split_number(dest)
    packed = dot_nt(stack_rows([high, low]), select)
    packed = (32.0 * packed[0:1] + packed[1:2]).astype(I32)
    place_ref[...] = ones_where(iota((tok, tok), 0) == packed)


def plan(modality, owner_ids, groups):
    tok = modality.shape[0]
    return pl.pallas_call(
        functools.partial(plan_kernel, groups),
        out_shape=jax.ShapeDtypeStruct((tok, tok), BF16),
        in_specs=[VMEM, VMEM],
        out_specs=VMEM,
        compiler_params=pltpu.CompilerParams(vmem_limit_bytes=24 * MIB),
        name="plan",
    )(modality, owner_ids)


def place_kernel(place_ref, keep_ref, got_ref, mine_ref, out_ref):
    own = jnp.concatenate([keep_ref[...], mine_ref[...]], axis=1)
    rows = jnp.concatenate([own, got_ref[...]], axis=0)
    out_ref[...] = dot(place_ref[...], rows).astype(BF16)


def place(where, keep, got, mine):
    tok = where.shape[0]
    return pl.pallas_call(
        place_kernel,
        out_shape=jax.ShapeDtypeStruct((tok, 3 * HD), BF16),
        in_specs=[VMEM] * 4,
        out_specs=VMEM,
        compiler_params=pltpu.CompilerParams(vmem_limit_bytes=16 * MIB),
        name="place",
    )(where, keep, got, mine)


def mask_kernel(note_ref, modality_ref, owner_ref, bias_ref, back_ref, notes, sem):
    groups, rows, cols = note_ref.shape
    tok = bias_ref.shape[0]
    slots = tok // groups
    copy = pltpu.make_async_copy(note_ref.at[:, pl.ds(rows - 16, 16)], notes, sem)
    copy.start()
    modality = row_of(modality_ref)
    dest, _ = slots_of(modality, row_of(owner_ref), groups)
    same = ones_where(iota((tok, tok), 0) == iota((tok, tok), 1))
    high, low = split_number(dest)
    mine = jnp.where(modality == lax.axis_index("tower"), 1.0, 0.0)
    back = dot_nt(same, stack_rows([high, low, mine]))
    dest = (32.0 * back[:, 0:1] + back[:, 1:2]).astype(I32)
    dest = jnp.where(back[:, 2:3] > 0.5, dest, -1)
    back_ref[...] = ones_where(iota((tok, tok), 1) == dest)

    copy.wait()
    group = lax.axis_index("grp")
    seen = notes[...].astype(F32)
    facts = jnp.concatenate([seen[:, :8], seen[:, 8:]], axis=2)[:, :, :tok]
    facts = facts.reshape(groups * 8, tok).astype(BF16)

    def part(index):
        return jnp.floor((index.astype(F32) + 0.5) * (1.0 / slots))

    column = iota((1, tok), 1)
    from_group = part(column)
    slot = column - slots * from_group.astype(I32)
    take = ones_where(iota((tok, tok), 0) == group * slots + slot)
    seen = dot(facts, take).reshape(groups, 8, tok)
    at = iota((groups, 8, tok), 0)
    row = jnp.sum(jnp.where(at == from_group.astype(I32)[None], seen, 0.0), axis=0)
    turned = dot_nt(same, row.astype(BF16))
    row_place = tok * from_group + 32.0 * row[1:2] + row[2:3]
    turned_place = tok * part(iota((tok, 1), 0)) + 32.0 * turned[:, 1:2] + turned[:, 2:3]
    after = (row_place <= turned_place) | (row[3:4] * turned[:, 3:4] > 0.5)
    allowed = (row[0:1] == turned[:, 0:1]) & after
    bias_ref[...] = jnp.where(allowed, 0.0, MASKED).astype(BF16)


def masks(weights, modality, owner_ids):
    tok = modality.shape[0]
    groups, _, cols = weights.shape
    return pl.pallas_call(
        mask_kernel,
        out_shape=(
            jax.ShapeDtypeStruct((tok, tok), BF16),
            jax.ShapeDtypeStruct((tok, tok), BF16),
        ),
        in_specs=[HBM, VMEM, VMEM],
        out_specs=(VMEM, VMEM),
        scratch_shapes=[pltpu.VMEM((groups, 16, cols), BF16), pltpu.SemaphoreType.DMA],
        compiler_params=pltpu.CompilerParams(vmem_limit_bytes=32 * MIB),
        name="masks",
    )(*in_hbm(weights), modality, owner_ids)


def attend_kernel(given_ref, bias_ref, out_ref):
    tok = given_ref.shape[0]
    keys, values = given_ref[:, HD : 2 * HD], given_ref[:, 2 * HD :]
    tile = min(256, tok)
    for at in range(0, tok, tile):
        scores = dot_nt(given_ref[at : at + tile, :HD], keys) * (math.log2(math.e) / math.sqrt(HD))
        scores = scores + bias_ref[at : at + tile, :].astype(F32)
        powered = jnp.exp2(scores - jnp.max(scores, axis=1, keepdims=True))
        inverse = 1.0 / jnp.sum(powered, axis=1, keepdims=True)
        mixed = dot((powered * inverse).astype(BF16), values).astype(BF16)
        out_ref[0, at : at + tile, :] = mixed
        out_ref[1, at : at + tile, :] = mixed


def attend(given, bias):
    tok = bias.shape[0]
    return pl.pallas_call(
        attend_kernel,
        out_shape=jax.ShapeDtypeStruct((2, tok, HD), BF16),
        in_specs=[VMEM, VMEM],
        out_specs=VMEM,
        compiler_params=pltpu.CompilerParams(vmem_limit_bytes=24 * MIB),
        name="attend",
    )(given, bias)


def restore_kernel(back_ref, given_ref, out_ref):
    both = jnp.concatenate([given_ref[0], given_ref[1]], axis=1)
    out_ref[0] = dot(back_ref[...], both).astype(BF16)


def restore(back, given):
    tok = back.shape[0]
    return pl.pallas_call(
        restore_kernel,
        out_shape=jax.ShapeDtypeStruct((1, tok, 2 * HD), BF16),
        in_specs=[VMEM, VMEM],
        out_specs=VMEM,
        compiler_params=pltpu.CompilerParams(vmem_limit_bytes=16 * MIB),
        name="restore",
    )(back, given)


def swap_all(value, axes):
    return lax.all_to_all(value, axes, split_axis=0, concat_axis=0, tiled=True)


def local(tokens, modality, doc_ids, owner_ids, norm_gain, query_weight, pair_weight):
    groups = lax.axis_size("grp")
    tok = tokens.shape[0]
    slots = tok // groups
    chosen, packed = pack(
        modality, owner_ids, doc_ids, tokens, query_weight, pair_weight, groups
    )
    weights = lax.all_gather(packed, "grp", axis=0)
    lifted = (chosen.astype(F32) * LIFT).astype(jnp.float16)
    gathered = lax.all_gather(lifted, "tp", axis=0)
    features = (gathered.astype(F32) * (1.0 / LIFT)).astype(BF16)
    keep, mine, give = project(normalize(features, norm_gain), weights)
    got = lax.ppermute(give, "tower", [(0, 1), (1, 0)])
    keep, later, owners = lax.optimization_barrier((keep, modality, owner_ids))
    sent = place(plan(later, owners, groups), keep, got, mine)
    sent, weights, later, owners = lax.optimization_barrier((sent, weights, later, owners))
    given = swap_all(sent.reshape(groups, slots, 3 * HD), "grp").reshape(tok, 3 * HD)
    bias, back = masks(weights, later, owners)
    mixed = attend(given, bias)
    returned = swap_all(mixed.reshape(2 * groups, slots, HD), ("tower", "grp"))
    return restore(back, returned.reshape(2, tok, HD))


def solution(mesh):
    in_specs = (
        P("grp", "tp"),
        P("grp"),
        P("grp"),
        P("grp"),
        P("tower", None),
        P("tower", "grp", "tp"),
        P("tower", "grp", None),
    )
    out_specs = P("tower", "grp", "tp")
    return jax.shard_map(local, mesh=mesh, in_specs=in_specs, out_specs=out_specs, check_vma=False)
```
